32 devices in a mesh: groups: 2 (over x), sensor: 8 (over z, y), seg: 2 (over core).
Axes of the slice: x: 2, y: 2, z: 4, core: 2. Of those that a mesh axis runs over, the one named last changes fastest.
Arguments:
- traces: bfloat16 [2, 512, 4096], P('seg', ('groups', 'sensor')), parts along dimension 1, may hold values from -40 to 40
- fir_taps: bfloat16 [512, 255], P(('groups', 'sensor')), parts along dimension 0, may hold values from -0.375 to 0.375
- slot_channel: int32 [16, 32], P(('groups', 'sensor')), parts along dimension 0, may hold values from 0 to 31, each once within a row
- segment_valid: int32 [2, 512], P('seg', ('groups', 'sensor')), parts along dimension 1, may hold values 0 or 1
- distances: int32 [2], replicated, may hold values from 1 to 7, as said below
Outputs:
- pair_sums: float32 [2, 512, 1536], P(None, ('groups', 'sensor'), 'seg'), parts along dimension 1
The draws below stay inside these ranges and needn't reach their ends.
There are 2 independent parts, one for each index of `groups`. The reference program is written for one: setup_inputs(seed, part) draws one part's arguments, and reference() takes and returns one part's arrays. A program takes and returns all parts, laid end to end along the dimension named above; an argument that names none is the same for every part. Nothing has to cross between parts.
Inputs may be any that keep to these rules, and one draw needn't show every extreme that they name: `slot_channel`: each row lists every slot index of a block once. `distances`: one entry, at a position drawn anew, is 7.
All inputs are finite; a program needn't handle non-finite values. No bound on the sum of `segment_valid` on one device may be relied on, other than what follows from the above.
Results may differ from the reference program's by a relative error of at most 0.004.
Values may be sent and summed in bfloat16 or wider, within the bound.
A program may use at most 64 MiB of HBM per device.

```python
import math
import jax
import jax.numpy as jnp
from jax import lax

CH_DEV = 32
SAMPLES = 4096
TAPS = 255
LAGS = 48
ROUNDS = 2
BLOCKS = 8
CHANNELS = 256
SEGS = 2


def draw_traces(key, part):
    key = jax.random.fold_in(key, 5)
    key_list = jax.random.split(key, 3)
    full_shape = (SEGS, CHANNELS, SAMPLES)
    noise_field = jnp.clip(jax.random.normal(key_list[0], full_shape, jnp.float32), -4.0, 4.0)
    spread = 1.15
    row_scale = jnp.exp(jax.random.uniform(key_list[1], (SEGS, CHANNELS, 1), jnp.float32, -spread, spread))
    envelope = jnp.exp(jax.random.uniform(key_list[2], (SEGS, CHANNELS, SAMPLES // 64, 1), jnp.float32, -1.0, 1.0))
    shaped = (noise_field * row_scale).reshape(SEGS, CHANNELS, SAMPLES // 64, 64) * envelope
    return shaped.reshape(full_shape).astype(jnp.bfloat16)


def draw_distances(key, part):
    key = jax.random.fold_in(key, 9)
    first_key, second_key = jax.random.split(key)
    picks = jax.random.randint(first_key, (ROUNDS,), 1, BLOCKS, dtype=jnp.int32)
    position = jax.random.randint(second_key, (), 0, ROUNDS, dtype=jnp.int32)
    return jnp.where(jnp.arange(ROUNDS, dtype=jnp.int32) == position, BLOCKS - 1, picks).astype(jnp.int32)


def touch_ends(result, stream_key, least, top_value):
    extent = result.shape
    place = [jax.random.randint(jax.random.fold_in(stream_key, axis), (), 0, extent[axis]) for axis in range(len(extent))]
    result = result.at[tuple(place)].set(least)
    longest = extent.index(max(extent))
    place[longest] = (place[longest] + 1) % extent[longest]
    return result.at[tuple(place)].set(top_value)


def levels(rng, extent, cuts, smallest, largest):
    factor_of, own = 1.0, jax.random.fold_in(rng, 6)
    for dim, blocks in cuts:
        steps = jnp.exp(jax.random.uniform(jax.random.fold_in(own, dim), (blocks,), jnp.float32, smallest / len(cuts), largest / len(cuts)))
        factor_of = factor_of * jnp.repeat(steps, extent[dim] // blocks).reshape([-1 if axis == dim else 1 for axis in range(len(extent))])
    return factor_of


def scatter_about(rng, shape, deviation, limit, shards=(), held_as=jnp.bfloat16):
    factor_of = levels(rng, shape, shards, -0.22, 0.18) if shards else 1.0
    result = jax.random.normal(rng, shape, jnp.float32) * deviation * factor_of
    return jnp.minimum(jnp.maximum(result, -limit), limit).astype(held_as)


def setup_inputs(seed: int = 0, part: int = 0) -> dict:
    streams_of = jax.random.split(jax.random.key(seed), 6)
    part_splits = jax.random.split(jax.random.fold_in(streams_of[5], part), 6)
    traces = draw_traces(jax.random.fold_in(jax.random.fold_in(streams_of[5], part), 71), part)
    fir_taps = scatter_about(part_splits[1], (CHANNELS, TAPS), TAPS ** -0.5, 0.375, ((0, 8),))
    slot_channel = jax.vmap(lambda own: jax.random.permutation(own, CH_DEV))(jax.random.split(part_splits[2], BLOCKS)).reshape((BLOCKS, CH_DEV)).astype(jnp.int32)
    segment_valid = touch_ends((jax.random.randint(part_splits[3], (SEGS, CHANNELS), 0, 4) < 3).astype(jnp.int32), jax.random.fold_in(part_splits[3], 1), 0, 1)
    distances = draw_distances(jax.random.fold_in(streams_of[5], 71), part)
    return dict(traces=traces, fir_taps=fir_taps, slot_channel=slot_channel, segment_valid=segment_valid, distances=distances)


epsilon = 1e-06

def whiten_rows(records, filter_taps, usable):
    margin = (filter_taps.shape[1] - 1) // 2
    filtered = lax.conv_general_dilated(records.astype(jnp.float32), filter_taps.astype(jnp.float32)[:, None, :], (1,), [(margin, margin)], dimension_numbers=('NCH', 'OIH', 'NCH'), feature_group_count=filter_taps.shape[0], precision=lax.Precision.HIGHEST)
    energy = lax.optimization_barrier(jnp.mean(filtered * filtered, axis=2, keepdims=True))
    scaled = filtered * lax.rsqrt(energy + epsilon) * usable[:, :, None].astype(jnp.float32)
    return scaled.astype(jnp.bfloat16)

def correlate_pair(left_rows, right_rows):
    sample_count = left_rows.shape[2]
    block_width = min(512, sample_count)
    before = LAGS // 2
    padded = jnp.pad(right_rows.astype(jnp.float32), ((0, 0), (0, 0), (before, LAGS - 1 - before)))
    left_f32 = left_rows.astype(jnp.float32)

    def advance(summed, block_index):
        offset = block_index * block_width
        left_piece = lax.dynamic_slice_in_dim(left_f32, offset, block_width, 2)
        window = lax.dynamic_slice_in_dim(padded, offset, block_width + LAGS - 1, 2)
        shifted = jnp.stack([window[:, :, lag_index:lag_index + block_width] for lag_index in range(LAGS)], axis=2)
        return (summed + jnp.einsum('sip,sjlp->ijl', left_piece, shifted, precision=lax.Precision.HIGHEST), None)
    start_sum = jnp.zeros((left_rows.shape[1], right_rows.shape[1], LAGS), jnp.float32)
    summed, _ = lax.scan(advance, start_sum, jnp.arange(sample_count // block_width, dtype=jnp.int32))
    return summed.reshape(left_rows.shape[1], right_rows.shape[1] * LAGS)

def reference(traces, fir_taps, slot_channel, segment_valid, distances):
    by_block = jnp.transpose(traces.reshape(SEGS, BLOCKS, CH_DEV, SAMPLES), (1, 0, 2, 3))
    taps_blocks = fir_taps.reshape(BLOCKS, CH_DEV, fir_taps.shape[1])
    usable_blocks = jnp.transpose(segment_valid.reshape(SEGS, BLOCKS, CH_DEV), (1, 0, 2))

    def whiten_block(pieces):
        records, filter_taps, usable, slot_order = pieces
        return jnp.take(whiten_rows(records, filter_taps, usable), slot_order, axis=1)
    whitened = lax.map(whiten_block, (by_block, taps_blocks, usable_blocks, slot_channel))
    factor = 1.0 / math.sqrt(SAMPLES * SEGS)
    results = []
    for round_index in range(ROUNDS):

        def pair_block(block_index):
            partner = jnp.bitwise_xor(block_index, distances[round_index])
            return correlate_pair(whitened[block_index], whitened[partner]) * factor
        per_block = lax.map(pair_block, jnp.arange(BLOCKS, dtype=jnp.int32))
        results.append(per_block.reshape(CHANNELS, CH_DEV * LAGS))
    return jnp.stack(results)
```

```python
import functools
import math

import jax
import jax.numpy as jnp
from jax import lax
from jax.experimental import pallas as pl
from jax.experimental.pallas import tpu as pltpu
from jax.sharding import PartitionSpec as P

LAGS = 48
FINE = 8
COARSE = LAGS // FINE
LANES = 128
EPSILON = 1e-06
NT = (((1,), (1,)), ((), ()))


def whiten_kernel(slot_ref, valid_ref, traces_ref, taps_ref, out_ref, rows_ref, taps_f32):
    channels, samples = traces_ref.shape[1:]
    tap_count = taps_ref.shape[1]
    pieces = samples // LANES
    margin = (tap_count - 1) // 2
    width = 3 * LANES
    rows_ref[0:channels] = jnp.zeros((channels, LANES), jnp.float32)
    rows_ref[(pieces + 1) * channels :] = jnp.zeros((channels, LANES), jnp.float32)
    for piece in range(pieces):
        rows_ref[(piece + 1) * channels : (piece + 2) * channels] = traces_ref[
            0, :, piece * LANES : (piece + 1) * LANES
        ].astype(jnp.float32)
    taps_f32[...] = jnp.zeros_like(taps_f32)
    taps_f32[:, 0:tap_count] = taps_ref[...].astype(jnp.float32)

    @pl.loop(0, channels, unroll=4)
    def _(slot):
        channel = slot_ref[0, slot]
        usable = valid_ref[0, channel].astype(jnp.float32)
        windows = jnp.concatenate(
            [
                rows_ref[pl.ds(piece * channels + channel, pieces, stride=channels)].astype(jnp.bfloat16)
                for piece in range(3)
            ],
            axis=1,
        )
        filter_row = jnp.broadcast_to(taps_f32[pl.ds(channel, 1)], (LANES, width))
        banded = pltpu.roll(filter_row, LANES - margin, 1, stride=1, stride_axis=0)
        filtered = lax.dot_general(
            windows, banded.astype(jnp.bfloat16), NT, preferred_element_type=jnp.float32
        )
        energy = jnp.sum(filtered * filtered, keepdims=True) * (1.0 / samples)
        scaled = filtered * (lax.rsqrt(energy + EPSILON) * usable)
        out_ref[pl.ds(slot, pieces, stride=channels)] = scaled


def shifted(now, following, amount):
    if amount == 0:
        return now
    lane = lax.broadcasted_iota(jnp.int32, now.shape, 1)
    rolled = [pltpu.roll(x, LANES - amount, 1) for x in (now, following)]
    return jnp.where(lane < LANES - amount, rolled[0], rolled[1])


def correlate_kernel(own_ref, first_ref, second_ref, out_ref, left_ref, right_ref):
    pieces, channels, _ = own_ref.shape
    half = channels // 2
    before = LAGS // 2
    zero = jnp.zeros((channels, LANES), jnp.float32)

    def piece_of(ref, piece):
        if piece < 0 or piece >= pieces:
            return zero
        return ref[piece].astype(jnp.float32)

    for piece in range(-1, pieces):
        lanes = slice((piece + 1) * LANES, (piece + 2) * LANES)
        for coarse in range(COARSE):
            amount = before - FINE * coarse
            if amount >= 0:
                value = shifted(piece_of(own_ref, piece), piece_of(own_ref, piece + 1), amount)
            else:
                value = shifted(piece_of(own_ref, piece - 1), piece_of(own_ref, piece), LANES + amount)
            left_ref[coarse * channels : (coarse + 1) * channels, lanes] = value.astype(jnp.bfloat16)
        for round_index, ref in enumerate((first_ref, second_ref)):
            for fine in range(FINE):
                value = shifted(piece_of(ref, piece), piece_of(ref, piece + 1), fine).astype(jnp.bfloat16)
                for part in range(2):
                    row = part * 2 * FINE * half + round_index * FINE * half + fine * half
                    right_ref[row : row + half, lanes] = value[part * half : (part + 1) * half]
    products = lax.dot_general(left_ref[...], right_ref[...], NT, preferred_element_type=jnp.float32)
    columns = products.shape[1] // 2
    out_ref[0] = products[:, :columns]
    out_ref[1] = products[:, columns:]


def arrange_kernel(factor, sums_ref, out_ref, table_ref):
    round_count, channels, columns = out_ref.shape
    half = channels // 2
    width = FINE * half
    for coarse in range(COARSE):
        row = lax.broadcasted_iota(jnp.int32, (width, columns), 0)
        column = lax.broadcasted_iota(jnp.int32, (width, columns), 1)
        target = (row % half) * LAGS + row // half + coarse * FINE
        table_ref[coarse * width : (coarse + 1) * width] = jnp.where(column == target, 1.0, 0.0).astype(jnp.bfloat16)
    gathered = jnp.concatenate(
        [
            jnp.concatenate(
                [
                    sums_ref[coarse * channels : (coarse + 1) * channels, r * width : (r + 1) * width]
                    for coarse in range(COARSE)
                ],
                axis=1,
            )
            for r in range(round_count)
        ],
        axis=0,
    ) * factor
    top = gathered.astype(jnp.bfloat16)
    rest = gathered - top.astype(jnp.float32)
    middle = rest.astype(jnp.bfloat16)
    low = (rest - middle.astype(jnp.float32)).astype(jnp.bfloat16)
    stacked = jnp.concatenate([top, middle, low], axis=0)
    moved = jnp.dot(stacked, table_ref[...], preferred_element_type=jnp.float32)
    count = round_count * channels
    result = moved[:count] + (moved[count : 2 * count] + moved[2 * count :])
    for r in range(round_count):
        out_ref[r] = result[r * channels : (r + 1) * channels]


def swapped(value, mask):
    pairs = [(source, source ^ mask) for source in range(lax.axis_size("sensor"))]
    return lax.ppermute(value, "sensor", pairs)


def shards(traces, fir_taps, slot_channel, segment_valid, distances):
    _, channels, samples = traces.shape
    pieces = samples // LANES
    half = channels // 2
    vmem = pl.BlockSpec(memory_space=pltpu.VMEM)
    smem = pl.BlockSpec(memory_space=pltpu.SMEM)
    params = pltpu.CompilerParams(vmem_limit_bytes=48 * 2**20)
    whitened = pl.pallas_call(
        whiten_kernel,
        out_shape=jax.ShapeDtypeStruct((pieces * channels, LANES), jnp.float32),
        in_specs=[smem, smem, vmem, vmem],
        out_specs=vmem,
        scratch_shapes=[
            pltpu.VMEM(((pieces + 2) * channels, LANES), jnp.float32),
            pltpu.VMEM((channels, 3 * LANES), jnp.float32),
        ],
        compiler_params=params,
    )(slot_channel, segment_valid, traces, fir_taps)
    whitened = whitened.astype(jnp.bfloat16).reshape(pieces, channels, LANES)

    blocks = lax.axis_size("sensor")
    farthest = blocks - 1
    opposite = swapped(whitened, farthest)
    first_far = distances[0] == farthest
    other = jnp.where(first_far, distances[1], distances[0])
    crosses = other >= blocks // 2
    carried = jnp.where(crosses, opposite, whitened)
    rest = jnp.where(crosses, jnp.bitwise_xor(other, farthest), other)
    for bit in range(farthest.bit_length() - 1):
        chosen = jnp.bitwise_and(jnp.right_shift(rest, bit), 1) == 1
        carried = jnp.where(chosen, swapped(carried, 1 << bit), carried)
    first = jnp.where(first_far, opposite, carried)
    second = jnp.where(first_far, carried, opposite)

    depth = (pieces + 1) * LANES
    products = pl.pallas_call(
        correlate_kernel,
        out_shape=jax.ShapeDtypeStruct((2, COARSE * channels, 2 * FINE * half), jnp.float32),
        in_specs=[vmem] * 3,
        out_specs=vmem,
        scratch_shapes=[
            pltpu.VMEM((COARSE * channels, depth), jnp.bfloat16),
            pltpu.VMEM((2 * FINE * channels, depth), jnp.bfloat16),
        ],
        compiler_params=params,
    )(whitened, first, second)
    summed = lax.psum_scatter(products, "seg", scatter_dimension=0, tiled=False)
    factor = 1.0 / math.sqrt(samples * traces.shape[0] * lax.axis_size("seg"))
    return pl.pallas_call(
        functools.partial(arrange_kernel, factor),
        out_shape=jax.ShapeDtypeStruct((2, channels, half * LAGS), jnp.float32),
        in_specs=[vmem],
        out_specs=vmem,
        scratch_shapes=[pltpu.VMEM((COARSE * FINE * half, half * LAGS), jnp.bfloat16)],
        compiler_params=params,
    )(summed)


def solution(mesh):
    placed = (
        P("seg", ("groups", "sensor"), None),
        P(("groups", "sensor"), None),
        P(("groups", "sensor"), None),
        P("seg", ("groups", "sensor")),
        P(),
    )
    return jax.shard_map(
        shards,
        mesh=mesh,
        in_specs=placed,
        out_specs=P(None, ("groups", "sensor"), "seg"),
        check_vma=False,
    )
```

```python
import functools
import math

import jax
import jax.numpy as jnp
from jax import lax
from jax.experimental import pallas as pl
from jax.experimental.pallas import tpu as pltpu
from jax.sharding import PartitionSpec as P

LAGS = 48
FINE = 8
COARSE = LAGS // FINE
LANES = 128
CHUNKS = 4
EPSILON = 1e-06
NT = (((1,), (1,)), ((), ()))


def whiten_kernel(
    slot_hbm, valid_hbm, traces_hbm, taps_hbm, out_ref, slot_ref, valid_ref, traces_ref, taps_ref,
    rows_ref, taps_f32, scaled_ref, sems,
):
    copies = [
        pltpu.make_async_copy(source, target, sems.at[index])
        for index, (source, target) in enumerate(
            [(traces_hbm, traces_ref), (taps_hbm, taps_ref), (slot_hbm, slot_ref), (valid_hbm, valid_ref)]
        )
    ]
    for copy in copies:
        copy.start()
    for copy in copies:
        copy.wait()
    channels, samples = traces_ref.shape[1:]
    tap_count = taps_ref.shape[1]
    pieces = samples // LANES
    margin = (tap_count - 1) // 2
    width = 3 * LANES
    rows_ref[0:channels] = jnp.zeros((channels, LANES), jnp.float32)
    rows_ref[(pieces + 1) * channels :] = jnp.zeros((channels, LANES), jnp.float32)
    for piece in range(pieces):
        rows_ref[(piece + 1) * channels : (piece + 2) * channels] = traces_ref[
            0, :, piece * LANES : (piece + 1) * LANES
        ].astype(jnp.float32)
    taps_f32[...] = jnp.zeros_like(taps_f32)
    taps_f32[:, 0:tap_count] = taps_ref[...].astype(jnp.float32)

    @pl.loop(0, channels, unroll=4)
    def _(slot):
        channel = slot_ref[0, slot]
        usable = valid_ref[0, channel].astype(jnp.float32)
        windows = jnp.concatenate(
            [
                rows_ref[pl.ds(piece * channels + channel, pieces, stride=channels)].astype(jnp.bfloat16)
                for piece in range(3)
            ],
            axis=1,
        )
        filter_row = jnp.broadcast_to(taps_f32[pl.ds(channel, 1)], (LANES, width))
        banded = pltpu.roll(filter_row, LANES - margin, 1, stride=1, stride_axis=0)
        filtered = lax.dot_general(
            windows, banded.astype(jnp.bfloat16), NT, preferred_element_type=jnp.float32
        )
        energy = jnp.sum(filtered * filtered, keepdims=True) * (1.0 / samples)
        scaled = filtered * (lax.rsqrt(energy + EPSILON) * usable)
        scaled_ref[pl.ds(slot, pieces, stride=channels)] = scaled

    for piece in range(pieces):
        out_ref[piece] = scaled_ref[piece * channels : (piece + 1) * channels].astype(jnp.bfloat16)


def shifted(now, following, amount):
    if amount == 0:
        return now
    lane = lax.broadcasted_iota(jnp.int32, now.shape, 1)
    rolled = [pltpu.roll(x, LANES - amount, 1) for x in (now, following)]
    return jnp.where(lane < LANES - amount, rolled[0], rolled[1])


def arrange(table_ref, parts, factor):
    rows = jnp.concatenate(parts, axis=0) * factor
    top = rows.astype(jnp.bfloat16)
    rest = rows - top.astype(jnp.float32)
    middle = rest.astype(jnp.bfloat16)
    low = (rest - middle.astype(jnp.float32)).astype(jnp.bfloat16)
    stacked = jnp.concatenate([top, middle, low], axis=0)
    moved = jnp.dot(stacked, table_ref[...], preferred_element_type=jnp.float32)
    count = rows.shape[0]
    return moved[:count] + (moved[count : 2 * count] + moved[2 * count :])


def exchange_kernel(
    blocks, factor, distances_ref, own_ref, out_ref, padded_ref, far_ref, carried_ref, arrived_ref,
    left_ref, right_ref, products_ref, sums_ref, table_ref, far_sems, hop_sems, sum_sems,
):
    pieces, channels, _ = own_ref.shape
    half = channels // 2
    before = LAGS // 2
    width = FINE * half
    farthest = blocks - 1
    hops = farthest.bit_length() - 1
    per_chunk = pieces // CHUNKS
    me = lax.axis_index("sensor")
    seg = lax.axis_index("seg")

    def partner(mask):
        result = 0
        for bit in range(farthest.bit_length()):
            value = lax.rem(lax.div(me, 1 << bit), 2)
            result = result + ((1 - value) if (mask >> bit) & 1 else value) * (1 << bit)
        return {"sensor": result}

    barrier = pltpu.get_barrier_semaphore()
    others = [partner(farthest)] + [partner(1 << bit) for bit in range(hops)] + [{"seg": 1 - seg}]
    for other in others:
        pl.semaphore_signal(barrier, inc=1, device_id=other, device_id_type=pl.DeviceIdType.MESH)
    pl.semaphore_wait(barrier, len(others))

    def far_copy(chunk):
        return pltpu.make_async_remote_copy(
            src_ref=own_ref.at[pl.ds(chunk * per_chunk, per_chunk)],
            dst_ref=far_ref.at[pl.ds(1 + chunk * per_chunk, per_chunk)],
            send_sem=far_sems.at[0, chunk],
            recv_sem=far_sems.at[1, chunk],
            device_id=others[0],
            device_id_type=pl.DeviceIdType.MESH,
        )

    def hop_copy(bit, chunk):
        return pltpu.make_async_remote_copy(
            src_ref=carried_ref.at[bit, pl.ds(1 + chunk * per_chunk, per_chunk)],
            dst_ref=arrived_ref.at[bit, pl.ds(chunk * per_chunk, per_chunk)],
            send_sem=hop_sems.at[0, bit, chunk],
            recv_sem=hop_sems.at[1, bit, chunk],
            device_id=others[1 + bit],
            device_id_type=pl.DeviceIdType.MESH,
        )

    def sum_copy(which):
        return pltpu.make_async_remote_copy(
            src_ref=products_ref.at[which, 1 - seg],
            dst_ref=sums_ref.at[which],
            send_sem=sum_sems.at[0, which],
            recv_sem=sum_sems.at[1, which],
            device_id=others[-1],
            device_id_type=pl.DeviceIdType.MESH,
        )

    for chunk in range(CHUNKS):
        far_copy(chunk).start()

    first_far = distances_ref[0] == farthest
    distance = jnp.where(first_far, distances_ref[1], distances_ref[0])
    crosses = distance >= blocks // 2
    remaining = jnp.where(crosses, farthest - distance, distance)

    edge = jnp.zeros((channels, LANES), jnp.bfloat16)
    padded_ref[0] = edge
    padded_ref[1] = edge
    padded_ref[pieces + 2] = edge
    far_ref[0] = edge
    far_ref[pieces + 1] = edge
    carried_ref[hops, 0] = edge
    carried_ref[hops, pieces + 1] = edge

    @pl.loop(0, pieces)
    def _(piece):
        padded_ref[piece + 2] = own_ref[piece]

    @pl.loop(0, pieces + 1)
    def _(piece):
        lanes = pl.ds(pl.multiple_of(piece * LANES, LANES), LANES)
        last, now, later = (padded_ref[piece + step].astype(jnp.float32) for step in range(3))
        for coarse in range(COARSE):
            amount = before - FINE * coarse
            if amount >= 0:
                value = shifted(now, later, amount)
            else:
                value = shifted(last, now, LANES + amount)
            left_ref[coarse * channels : (coarse + 1) * channels, lanes] = value.astype(jnp.bfloat16)

    for coarse in range(COARSE):
        row = lax.broadcasted_iota(jnp.int32, table_ref.shape[1:], 0)
        column = lax.broadcasted_iota(jnp.int32, table_ref.shape[1:], 1)
        target = (row & (half - 1)) * LAGS + (row >> (half.bit_length() - 1)) + coarse * FINE
        table_ref[coarse] = jnp.where(column == target, 1.0, 0.0).astype(jnp.bfloat16)

    def multiply(which, load, chunk):
        start = chunk * per_chunk
        count = per_chunk + (1 if chunk == CHUNKS - 1 else 0)

        @pl.loop(0, count)
        def _(step):
            lanes = pl.ds(pl.multiple_of(step * LANES, LANES), LANES)
            now, later = (load(start + step + ahead).astype(jnp.float32) for ahead in range(2))
            for fine in range(FINE):
                value = shifted(now, later, fine).astype(jnp.bfloat16)
                for part in range(2):
                    row = part * width + fine * half
                    right_ref[row : row + half, lanes] = value[part * half : (part + 1) * half]

        product = lax.dot_general(
            left_ref[:, start * LANES : (start + count) * LANES],
            right_ref[:, : count * LANES],
            NT,
            preferred_element_type=jnp.float32,
        )
        for part in range(2):
            addend = product[:, part * width : (part + 1) * width]
            if chunk == 0:
                products_ref[which, part] = addend
            else:
                products_ref[which, part] += addend

    for step in range(CHUNKS + hops):
        for stage in range(hops, -1, -1):
            chunk = step - stage
            if chunk < 0 or chunk >= CHUNKS:
                continue
            inside = pl.ds(1 + chunk * per_chunk, per_chunk)
            plain = pl.ds(chunk * per_chunk, per_chunk)
            if stage == 0:
                far_copy(chunk).wait_recv()
                carried_ref[0, inside] = lax.select(crosses, far_ref[inside], own_ref[plain])
            else:
                hop_copy(stage - 1, chunk).wait_recv()
                chosen = jnp.bitwise_and(jnp.right_shift(remaining, stage - 1), 1) == 1
                carried_ref[stage, inside] = lax.select(
                    chosen, arrived_ref[stage - 1, plain], carried_ref[stage - 1, inside]
                )
            if stage < hops:
                hop_copy(stage, chunk).start()
        if step < CHUNKS:
            multiply(0, lambda index: far_ref[index], step)
            if step == CHUNKS - 1:
                sum_copy(0).start()
        if step >= hops:
            multiply(1, lambda index: carried_ref[hops, index], step - hops)
    sum_copy(1).start()

    def gathered(which):
        total = products_ref[which, seg] + sums_ref[which]
        return jnp.concatenate(
            [total[coarse * channels : (coarse + 1) * channels] for coarse in range(COARSE)], axis=1
        )

    table = table_ref.reshape(COARSE * width, half * LAGS)
    sum_copy(0).wait_recv()
    from_far = arrange(table, [gathered(0)], factor)
    sum_copy(1).wait_recv()
    from_carried = arrange(table, [gathered(1)], factor)
    out_ref[0] = lax.select(first_far, from_far, from_carried)
    out_ref[1] = lax.select(first_far, from_carried, from_far)
    for chunk in range(CHUNKS):
        far_copy(chunk).wait_send()
        for bit in range(hops):
            hop_copy(bit, chunk).wait_send()
    for which in range(2):
        sum_copy(which).wait_send()


def shards(traces, fir_taps, slot_channel, segment_valid, distances):
    _, channels, samples = traces.shape
    pieces = samples // LANES
    half = channels // 2
    width = FINE * half
    vmem = pl.BlockSpec(memory_space=pltpu.VMEM)
    smem = pl.BlockSpec(memory_space=pltpu.SMEM)
    hbm = pl.BlockSpec(memory_space=pltpu.HBM)
    params = pltpu.CompilerParams(vmem_limit_bytes=48 * 2**20)
    whitened = pl.pallas_call(
        whiten_kernel,
        out_shape=jax.ShapeDtypeStruct((pieces, channels, LANES), jnp.bfloat16),
        in_specs=[hbm] * 4,
        out_specs=vmem,
        scratch_shapes=[
            pltpu.SMEM(slot_channel.shape, jnp.int32),
            pltpu.SMEM(segment_valid.shape, jnp.int32),
            pltpu.VMEM(traces.shape, jnp.bfloat16),
            pltpu.VMEM(fir_taps.shape, jnp.bfloat16),
            pltpu.VMEM(((pieces + 2) * channels, LANES), jnp.float32),
            pltpu.VMEM((channels, 3 * LANES), jnp.float32),
            pltpu.VMEM((pieces * channels, LANES), jnp.float32),
            pltpu.SemaphoreType.DMA((4,)),
        ],
        compiler_params=params,
    )(slot_channel, segment_valid, traces, fir_taps)

    blocks = lax.axis_size("sensor")
    hops = (blocks - 1).bit_length() - 1
    factor = 1.0 / math.sqrt(samples * traces.shape[0] * lax.axis_size("seg"))
    depth = (pieces + 1) * LANES
    return pl.pallas_call(
        functools.partial(exchange_kernel, blocks, factor),
        out_shape=jax.ShapeDtypeStruct((2, channels, half * LAGS), jnp.float32),
        in_specs=[smem, vmem],
        out_specs=vmem,
        scratch_shapes=[
            pltpu.VMEM((pieces + 3, channels, LANES), jnp.bfloat16),
            pltpu.VMEM((pieces + 2, channels, LANES), jnp.bfloat16),
            pltpu.VMEM((hops + 1, pieces + 2, channels, LANES), jnp.bfloat16),
            pltpu.VMEM((hops, pieces, channels, LANES), jnp.bfloat16),
            pltpu.VMEM((COARSE * channels, depth), jnp.bfloat16),
            pltpu.VMEM((2 * width, (pieces // CHUNKS + 1) * LANES), jnp.bfloat16),
            pltpu.VMEM((2, 2, COARSE * channels, width), jnp.float32),
            pltpu.VMEM((2, COARSE * channels, width), jnp.float32),
            pltpu.VMEM((COARSE, width, half * LAGS), jnp.bfloat16),
            pltpu.SemaphoreType.DMA((2, CHUNKS)),
            pltpu.SemaphoreType.DMA((2, hops, CHUNKS)),
            pltpu.SemaphoreType.DMA((2, 2)),
        ],
        compiler_params=pltpu.CompilerParams(
            collective_id=0, has_side_effects=True, vmem_limit_bytes=48 * 2**20
        ),
    )(distances, whitened)


def solution(mesh):
    placed = (
        P("seg", ("groups", "sensor"), None),
        P(("groups", "sensor"), None),
        P(("groups", "sensor"), None),
        P("seg", ("groups", "sensor")),
        P(),
    )
    return jax.shard_map(
        shards,
        mesh=mesh,
        in_specs=placed,
        out_specs=P(None, ("groups", "sensor"), "seg"),
        check_vma=False,
    )
```

```python
import functools
import math

import jax
import jax.numpy as jnp
from jax import lax
from jax.experimental import pallas as pl
from jax.experimental.pallas import tpu as pltpu
from jax.sharding import PartitionSpec as P

LAGS = 48
FINE = 8
COARSE = LAGS // FINE
LANES = 128
CHUNKS = 4
SLACK = 2
EPSILON = 1e-06
NT = (((1,), (1,)), ((), ()))


def whiten_kernel(
    slot_hbm, valid_hbm, traces_hbm, taps_hbm, out_ref, slot_ref, valid_ref, traces_ref, taps_ref,
    rows_ref, taps_f32, scaled_ref, sems,
):
    copies = [
        pltpu.make_async_copy(source, target, sems.at[index])
        for index, (source, target) in enumerate(
            [(traces_hbm, traces_ref), (taps_hbm, taps_ref), (slot_hbm, slot_ref), (valid_hbm, valid_ref)]
        )
    ]
    for copy in copies:
        copy.start()
    for copy in copies:
        copy.wait()
    channels, samples = traces_ref.shape[1:]
    tap_count = taps_ref.shape[1]
    pieces = samples // LANES
    margin = (tap_count - 1) // 2
    width = 3 * LANES
    rows_ref[0:channels] = jnp.zeros((channels, LANES), jnp.float32)
    rows_ref[(pieces + 1) * channels :] = jnp.zeros((channels, LANES), jnp.float32)
    for piece in range(pieces):
        rows_ref[(piece + 1) * channels : (piece + 2) * channels] = traces_ref[
            0, :, piece * LANES : (piece + 1) * LANES
        ].astype(jnp.float32)
    taps_f32[...] = jnp.zeros_like(taps_f32)
    taps_f32[:, 0:tap_count] = taps_ref[...].astype(jnp.float32)

    @pl.loop(0, channels, unroll=4)
    def _(slot):
        channel = slot_ref[0, slot]
        usable = valid_ref[0, channel].astype(jnp.float32)
        windows = jnp.concatenate(
            [
                rows_ref[pl.ds(piece * channels + channel, pieces, stride=channels)].astype(jnp.bfloat16)
                for piece in range(3)
            ],
            axis=1,
        )
        filter_row = jnp.broadcast_to(taps_f32[pl.ds(channel, 1)], (LANES, width))
        banded = pltpu.roll(filter_row, LANES - margin, 1, stride=1, stride_axis=0)
        filtered = lax.dot_general(
            windows, banded.astype(jnp.bfloat16), NT, preferred_element_type=jnp.float32
        )
        energy = jnp.sum(filtered * filtered, keepdims=True) * (1.0 / samples)
        scaled = filtered * (lax.rsqrt(energy + EPSILON) * usable)
        scaled_ref[pl.ds(slot, pieces, stride=channels)] = scaled

    for piece in range(pieces):
        out_ref[piece] = scaled_ref[piece * channels : (piece + 1) * channels].astype(jnp.bfloat16)


def shifted(now, following, amount):
    if amount == 0:
        return now
    lane = lax.broadcasted_iota(jnp.int32, now.shape, 1)
    rolled = [pltpu.roll(x, LANES - amount, 1) for x in (now, following)]
    return jnp.where(lane < LANES - amount, rolled[0], rolled[1])


def arrange(table_ref, parts, factor):
    rows = jnp.concatenate(parts, axis=0) * factor
    top = rows.astype(jnp.bfloat16)
    rest = rows - top.astype(jnp.float32)
    middle = rest.astype(jnp.bfloat16)
    low = (rest - middle.astype(jnp.float32)).astype(jnp.bfloat16)
    stacked = jnp.concatenate([top, middle, low], axis=0)
    moved = jnp.dot(stacked, table_ref[...], preferred_element_type=jnp.float32)
    count = rows.shape[0]
    return moved[:count] + (moved[count : 2 * count] + moved[2 * count :])


def exchange_kernel(
    blocks, factor, distances_ref, own_ref, out_ref, padded_ref, far_ref, carried_ref, arrived_ref,
    left_ref, right_ref, products_ref, sums_ref, table_ref, far_sems, hop_sems, sum_sems,
):
    pieces, channels, _ = own_ref.shape
    half = channels // 2
    before = LAGS // 2
    width = FINE * half
    farthest = blocks - 1
    hops = farthest.bit_length() - 1
    per_chunk = pieces // CHUNKS
    me = lax.axis_index("sensor")
    seg = lax.axis_index("seg")

    def partner(mask):
        result = 0
        for bit in range(farthest.bit_length()):
            value = lax.rem(lax.div(me, 1 << bit), 2)
            result = result + ((1 - value) if (mask >> bit) & 1 else value) * (1 << bit)
        return {"sensor": result}

    barrier = pltpu.get_barrier_semaphore()
    others = [partner(farthest)] + [partner(1 << bit) for bit in range(hops)] + [{"seg": 1 - seg}]
    for other in others:
        pl.semaphore_signal(barrier, inc=1, device_id=other, device_id_type=pl.DeviceIdType.MESH)
    pl.semaphore_wait(barrier, len(others))

    def far_copy(chunk):
        return pltpu.make_async_remote_copy(
            src_ref=own_ref.at[pl.ds(chunk * per_chunk, per_chunk)],
            dst_ref=far_ref.at[pl.ds(1 + chunk * per_chunk, per_chunk)],
            send_sem=far_sems.at[0, chunk],
            recv_sem=far_sems.at[1, chunk],
            device_id=others[0],
            device_id_type=pl.DeviceIdType.MESH,
        )

    def hop_copy(bit, chunk):
        return pltpu.make_async_remote_copy(
            src_ref=carried_ref.at[bit, pl.ds(1 + chunk * per_chunk, per_chunk)],
            dst_ref=arrived_ref.at[bit, pl.ds(chunk * per_chunk, per_chunk)],
            send_sem=hop_sems.at[0, bit, chunk],
            recv_sem=hop_sems.at[1, bit, chunk],
            device_id=others[1 + bit],
            device_id_type=pl.DeviceIdType.MESH,
        )

    def sum_copy(which):
        return pltpu.make_async_remote_copy(
            src_ref=products_ref.at[which, 1 - seg],
            dst_ref=sums_ref.at[which],
            send_sem=sum_sems.at[0, which],
            recv_sem=sum_sems.at[1, which],
            device_id=others[-1],
            device_id_type=pl.DeviceIdType.MESH,
        )

    for chunk in range(min(2, CHUNKS)):
        far_copy(chunk).start()

    first_far = distances_ref[0] == farthest
    distance = jnp.where(first_far, distances_ref[1], distances_ref[0])
    crosses = distance >= blocks // 2
    remaining = jnp.where(crosses, farthest - distance, distance)

    edge = jnp.zeros((channels, LANES), jnp.bfloat16)
    padded_ref[0] = edge
    padded_ref[1] = edge
    padded_ref[pieces + 2] = edge
    far_ref[0] = edge
    far_ref[pieces + 1] = edge
    carried_ref[hops, 0] = edge
    carried_ref[hops, pieces + 1] = edge

    @pl.loop(0, pieces)
    def _(piece):
        padded_ref[piece + 2] = own_ref[piece]

    @pl.loop(0, pieces + 1, unroll=3)
    def _(piece):
        lanes = pl.ds(pl.multiple_of(piece * LANES, LANES), LANES)
        last, now, later = (padded_ref[piece + step].astype(jnp.float32) for step in range(3))
        for coarse in range(COARSE):
            amount = before - FINE * coarse
            if amount >= 0:
                value = shifted(now, later, amount)
            else:
                value = shifted(last, now, LANES + amount)
            left_ref[coarse * channels : (coarse + 1) * channels, lanes] = value.astype(jnp.bfloat16)

    for coarse in range(COARSE):
        row = lax.broadcasted_iota(jnp.int32, table_ref.shape[1:], 0)
        column = lax.broadcasted_iota(jnp.int32, table_ref.shape[1:], 1)
        target = (row & (half - 1)) * LAGS + (row >> (half.bit_length() - 1)) + coarse * FINE
        table_ref[coarse] = jnp.where(column == target, 1.0, 0.0).astype(jnp.bfloat16)

    def multiply(which, load, chunk):
        start = chunk * per_chunk
        count = per_chunk + (1 if chunk == CHUNKS - 1 else 0)

        @pl.loop(0, count, unroll=count)
        def _(step):
            lanes = pl.ds(pl.multiple_of(step * LANES, LANES), LANES)
            now, later = (load(start + step + ahead).astype(jnp.float32) for ahead in range(2))
            for fine in range(FINE):
                value = shifted(now, later, fine).astype(jnp.bfloat16)
                for part in range(2):
                    row = part * width + fine * half
                    right_ref[row : row + half, lanes] = value[part * half : (part + 1) * half]

        product = lax.dot_general(
            left_ref[:, start * LANES : (start + count) * LANES],
            right_ref[:, : count * LANES],
            NT,
            preferred_element_type=jnp.float32,
        )
        for part in range(2):
            addend = product[:, part * width : (part + 1) * width]
            if chunk == 0:
                products_ref[which, part] = addend
            else:
                products_ref[which, part] += addend

    for step in range(CHUNKS + SLACK * hops):
        for stage in range(hops, -1, -1):
            chunk = step - SLACK * stage
            if chunk < 0 or chunk >= CHUNKS:
                continue
            inside = pl.ds(1 + chunk * per_chunk, per_chunk)
            plain = pl.ds(chunk * per_chunk, per_chunk)
            if stage == 0:
                far_copy(chunk).wait_recv()
                carried_ref[0, inside] = lax.select(crosses, far_ref[inside], own_ref[plain])
            else:
                hop_copy(stage - 1, chunk).wait_recv()
                chosen = jnp.bitwise_and(jnp.right_shift(remaining, stage - 1), 1) == 1
                carried_ref[stage, inside] = lax.select(
                    chosen, arrived_ref[stage - 1, plain], carried_ref[stage - 1, inside]
                )
            if stage < hops:
                hop_copy(stage, chunk).start()
            if stage == 0 and chunk + 2 < CHUNKS:
                far_copy(chunk + 2).start()
        if step < CHUNKS:
            multiply(0, lambda index: far_ref[index], step)
            if step == CHUNKS - 1:
                sum_copy(0).start()
        if step >= SLACK * hops:
            multiply(1, lambda index: carried_ref[hops, index], step - SLACK * hops)
    sum_copy(1).start()

    def gathered(which):
        total = products_ref[which, seg] + sums_ref[which]
        return jnp.concatenate(
            [total[coarse * channels : (coarse + 1) * channels] for coarse in range(COARSE)], axis=1
        )

    table = table_ref.reshape(COARSE * width, half * LAGS)
    sum_copy(0).wait_recv()
    from_far = arrange(table, [gathered(0)], factor)
    sum_copy(1).wait_recv()
    from_carried = arrange(table, [gathered(1)], factor)
    out_ref[0] = lax.select(first_far, from_far, from_carried)
    out_ref[1] = lax.select(first_far, from_carried, from_far)
    for chunk in range(CHUNKS):
        far_copy(chunk).wait_send()
        for bit in range(hops):
            hop_copy(bit, chunk).wait_send()
    for which in range(2):
        sum_copy(which).wait_send()


def shards(traces, fir_taps, slot_channel, segment_valid, distances):
    _, channels, samples = traces.shape
    pieces = samples // LANES
    half = channels // 2
    width = FINE * half
    vmem = pl.BlockSpec(memory_space=pltpu.VMEM)
    smem = pl.BlockSpec(memory_space=pltpu.SMEM)
    hbm = pl.BlockSpec(memory_space=pltpu.HBM)
    params = pltpu.CompilerParams(vmem_limit_bytes=64 * 2**20 - 2**17)
    whitened = pl.pallas_call(
        whiten_kernel,
        out_shape=jax.ShapeDtypeStruct((pieces, channels, LANES), jnp.bfloat16),
        in_specs=[hbm] * 4,
        out_specs=vmem,
        scratch_shapes=[
            pltpu.SMEM(slot_channel.shape, jnp.int32),
            pltpu.SMEM(segment_valid.shape, jnp.int32),
            pltpu.VMEM(traces.shape, jnp.bfloat16),
            pltpu.VMEM(fir_taps.shape, jnp.bfloat16),
            pltpu.VMEM(((pieces + 2) * channels, LANES), jnp.float32),
            pltpu.VMEM((channels, 3 * LANES), jnp.float32),
            pltpu.VMEM((pieces * channels, LANES), jnp.float32),
            pltpu.SemaphoreType.DMA((4,)),
        ],
        compiler_params=params,
    )(slot_channel, segment_valid, traces, fir_taps)

    blocks = lax.axis_size("sensor")
    hops = (blocks - 1).bit_length() - 1
    factor = 1.0 / math.sqrt(samples * traces.shape[0] * lax.axis_size("seg"))
    depth = (pieces + 1) * LANES
    return pl.pallas_call(
        functools.partial(exchange_kernel, blocks, factor),
        out_shape=jax.ShapeDtypeStruct((2, channels, half * LAGS), jnp.float32),
        in_specs=[smem, vmem],
        out_specs=vmem,
        scratch_shapes=[
            pltpu.VMEM((pieces + 3, channels, LANES), jnp.bfloat16),
            pltpu.VMEM((pieces + 2, channels, LANES), jnp.bfloat16),
            pltpu.VMEM((hops + 1, pieces + 2, channels, LANES), jnp.bfloat16),
            pltpu.VMEM((hops, pieces, channels, LANES), jnp.bfloat16),
            pltpu.VMEM((COARSE * channels, depth), jnp.bfloat16),
            pltpu.VMEM((2 * width, (pieces // CHUNKS + 1) * LANES), jnp.bfloat16),
            pltpu.VMEM((2, 2, COARSE * channels, width), jnp.float32),
            pltpu.VMEM((2, COARSE * channels, width), jnp.float32),
            pltpu.VMEM((COARSE, width, half * LAGS), jnp.bfloat16),
            pltpu.SemaphoreType.DMA((2, CHUNKS)),
            pltpu.SemaphoreType.DMA((2, hops, CHUNKS)),
            pltpu.SemaphoreType.DMA((2, 2)),
        ],
        compiler_params=pltpu.CompilerParams(
            collective_id=0, has_side_effects=True, vmem_limit_bytes=48 * 2**20
        ),
    )(distances, whitened)


def solution(mesh):
    placed = (
        P("seg", ("groups", "sensor"), None),
        P(("groups", "sensor"), None),
        P(("groups", "sensor"), None),
        P("seg", ("groups", "sensor")),
        P(),
    )
    return jax.shard_map(
        shards,
        mesh=mesh,
        in_specs=placed,
        out_specs=P(None, ("groups", "sensor"), "seg"),
        check_vma=False,
    )
```

```python
import functools
import math

import jax
import jax.numpy as jnp
from jax import lax
from jax.experimental import pallas as pl
from jax.experimental.pallas import tpu as pltpu
from jax.sharding import PartitionSpec as P

LAGS = 48
FINE = 8
COARSE = LAGS // FINE
LANES = 128
CHUNKS = 4
SLACK = 3
EPSILON = 1e-06
NT = (((1,), (1,)), ((), ()))


def whiten_kernel(
    slot_hbm, valid_hbm, traces_hbm, taps_hbm, out_ref, slot_ref, valid_ref, traces_ref, taps_ref,
    rows_ref, taps_f32, scaled_ref, sems,
):
    copies = [
        pltpu.make_async_copy(source, target, sems.at[index])
        for index, (source, target) in enumerate(
            [(traces_hbm, traces_ref), (taps_hbm, taps_ref), (slot_hbm, slot_ref), (valid_hbm, valid_ref)]
        )
    ]
    for copy in copies:
        copy.start()
    for copy in copies:
        copy.wait()
    channels, samples = traces_ref.shape[1:]
    tap_count = taps_ref.shape[1]
    pieces = samples // LANES
    margin = (tap_count - 1) // 2
    width = 3 * LANES
    rows_ref[0:channels] = jnp.zeros((channels, LANES), jnp.float32)
    rows_ref[(pieces + 1) * channels :] = jnp.zeros((channels, LANES), jnp.float32)
    for piece in range(pieces):
        rows_ref[(piece + 1) * channels : (piece + 2) * channels] = traces_ref[
            0, :, piece * LANES : (piece + 1) * LANES
        ].astype(jnp.float32)
    taps_f32[...] = jnp.zeros_like(taps_f32)
    taps_f32[:, 0:tap_count] = taps_ref[...].astype(jnp.float32)

    @pl.loop(0, channels, unroll=4)
    def _(slot):
        channel = slot_ref[0, slot]
        usable = valid_ref[0, channel].astype(jnp.float32)
        windows = jnp.concatenate(
            [
                rows_ref[pl.ds(piece * channels + channel, pieces, stride=channels)].astype(jnp.bfloat16)
                for piece in range(3)
            ],
            axis=1,
        )
        filter_row = jnp.broadcast_to(taps_f32[pl.ds(channel, 1)], (LANES, width))
        banded = pltpu.roll(filter_row, LANES - margin, 1, stride=1, stride_axis=0)
        filtered = lax.dot_general(
            windows, banded.astype(jnp.bfloat16), NT, preferred_element_type=jnp.float32
        )
        energy = jnp.sum(filtered * filtered, keepdims=True) * (1.0 / samples)
        scaled = filtered * (lax.rsqrt(energy + EPSILON) * usable)
        scaled_ref[pl.ds(slot, pieces, stride=channels)] = scaled

    for piece in range(pieces):
        out_ref[piece] = scaled_ref[piece * channels : (piece + 1) * channels].astype(jnp.bfloat16)


def shifted(now, following, amount):
    if amount == 0:
        return now
    lane = lax.broadcasted_iota(jnp.int32, now.shape, 1)
    rolled = [pltpu.roll(x, LANES - amount, 1) for x in (now, following)]
    return jnp.where(lane < LANES - amount, rolled[0], rolled[1])


def arrange(table_ref, parts, factor):
    rows = jnp.concatenate(parts, axis=0) * factor
    top = rows.astype(jnp.bfloat16)
    rest = rows - top.astype(jnp.float32)
    middle = rest.astype(jnp.bfloat16)
    low = (rest - middle.astype(jnp.float32)).astype(jnp.bfloat16)
    stacked = jnp.concatenate([top, middle, low], axis=0)
    moved = jnp.dot(stacked, table_ref[...], preferred_element_type=jnp.float32)
    count = rows.shape[0]
    return moved[:count] + (moved[count : 2 * count] + moved[2 * count :])


def exchange_kernel(
    blocks, factor, distances_ref, own_ref, out_ref, padded_ref, far_ref, carried_ref, arrived_ref,
    left_ref, right_ref, products_ref, sums_ref, table_ref, far_sems, hop_sems, sum_sems,
):
    pieces, channels, _ = own_ref.shape
    half = channels // 2
    before = LAGS // 2
    width = FINE * half
    farthest = blocks - 1
    hops = farthest.bit_length() - 1
    per_chunk = pieces // CHUNKS
    me = lax.axis_index("sensor")
    seg = lax.axis_index("seg")

    def partner(mask):
        result = 0
        for bit in range(farthest.bit_length()):
            value = lax.rem(lax.div(me, 1 << bit), 2)
            result = result + ((1 - value) if (mask >> bit) & 1 else value) * (1 << bit)
        return {"sensor": result}

    barrier = pltpu.get_barrier_semaphore()
    others = [partner(farthest)] + [partner(1 << bit) for bit in range(hops)] + [{"seg": 1 - seg}]
    for other in others:
        pl.semaphore_signal(barrier, inc=1, device_id=other, device_id_type=pl.DeviceIdType.MESH)
    pl.semaphore_wait(barrier, len(others))

    def far_copy(chunk):
        return pltpu.make_async_remote_copy(
            src_ref=own_ref.at[pl.ds(chunk * per_chunk, per_chunk)],
            dst_ref=far_ref.at[pl.ds(1 + chunk * per_chunk, per_chunk)],
            send_sem=far_sems.at[0, chunk],
            recv_sem=far_sems.at[1, chunk],
            device_id=others[0],
            device_id_type=pl.DeviceIdType.MESH,
        )

    def hop_partner(bit):
        up, down = others[1 + bit]["sensor"], others[hops - bit]["sensor"]
        return {"sensor": up + seg * (down - up)}

    def hop_copy(bit, chunk):
        return pltpu.make_async_remote_copy(
            src_ref=carried_ref.at[bit, pl.ds(1 + chunk * per_chunk, per_chunk)],
            dst_ref=arrived_ref.at[bit, pl.ds(chunk * per_chunk, per_chunk)],
            send_sem=hop_sems.at[0, bit, chunk],
            recv_sem=hop_sems.at[1, bit, chunk],
            device_id=hop_partner(bit),
            device_id_type=pl.DeviceIdType.MESH,
        )

    def sum_copy(which):
        return pltpu.make_async_remote_copy(
            src_ref=products_ref.at[which, 1 - seg],
            dst_ref=sums_ref.at[which],
            send_sem=sum_sems.at[0, which],
            recv_sem=sum_sems.at[1, which],
            device_id=others[-1],
            device_id_type=pl.DeviceIdType.MESH,
        )

    for chunk in range(min(2, CHUNKS)):
        far_copy(chunk).start()

    first_far = distances_ref[0] == farthest
    distance = jnp.where(first_far, distances_ref[1], distances_ref[0])
    crosses = distance >= blocks // 2
    remaining = jnp.where(crosses, farthest - distance, distance)

    edge = jnp.zeros((channels, LANES), jnp.bfloat16)
    padded_ref[0] = edge
    padded_ref[1] = edge
    padded_ref[pieces + 2] = edge
    far_ref[0] = edge
    far_ref[pieces + 1] = edge
    carried_ref[hops, 0] = edge
    carried_ref[hops, pieces + 1] = edge

    @pl.loop(0, pieces)
    def _(piece):
        padded_ref[piece + 2] = own_ref[piece]

    @pl.loop(0, pieces + 1, unroll=3)
    def _(piece):
        lanes = pl.ds(pl.multiple_of(piece * LANES, LANES), LANES)
        last, now, later = (padded_ref[piece + step].astype(jnp.float32) for step in range(3))
        for coarse in range(COARSE):
            amount = before - FINE * coarse
            if amount >= 0:
                value = shifted(now, later, amount)
            else:
                value = shifted(last, now, LANES + amount)
            left_ref[coarse * channels : (coarse + 1) * channels, lanes] = value.astype(jnp.bfloat16)

    for coarse in range(COARSE):
        row = lax.broadcasted_iota(jnp.int32, table_ref.shape[1:], 0)
        column = lax.broadcasted_iota(jnp.int32, table_ref.shape[1:], 1)
        target = (row & (half - 1)) * LAGS + (row >> (half.bit_length() - 1)) + coarse * FINE
        table_ref[coarse] = jnp.where(column == target, 1.0, 0.0).astype(jnp.bfloat16)

    def multiply(which, load, chunk):
        start = chunk * per_chunk
        count = per_chunk + (1 if chunk == CHUNKS - 1 else 0)

        @pl.loop(0, count, unroll=count)
        def _(step):
            lanes = pl.ds(pl.multiple_of(step * LANES, LANES), LANES)
            now, later = (load(start + step + ahead).astype(jnp.float32) for ahead in range(2))
            for fine in range(FINE):
                value = shifted(now, later, fine).astype(jnp.bfloat16)
                for part in range(2):
                    row = part * width + fine * half
                    right_ref[row : row + half, lanes] = value[part * half : (part + 1) * half]

        product = lax.dot_general(
            left_ref[:, start * LANES : (start + count) * LANES],
            right_ref[:, : count * LANES],
            NT,
            preferred_element_type=jnp.float32,
        )
        for part in range(2):
            addend = product[:, part * width : (part + 1) * width]
            if chunk == 0:
                products_ref[which, part] = addend
            else:
                products_ref[which, part] += addend

    for step in range(CHUNKS + SLACK * hops):
        for stage in range(hops, -1, -1):
            chunk = step - SLACK * stage
            if chunk < 0 or chunk >= CHUNKS:
                continue
            inside = pl.ds(1 + chunk * per_chunk, per_chunk)
            plain = pl.ds(chunk * per_chunk, per_chunk)
            if stage == 0:
                far_copy(chunk).wait_recv()
                carried_ref[0, inside] = lax.select(crosses, far_ref[inside], own_ref[plain])
            else:
                hop_copy(stage - 1, chunk).wait_recv()
                chosen = jnp.bitwise_and(jnp.right_shift(remaining, stage - 1 + seg * (hops + 1 - 2 * stage)), 1) == 1
                carried_ref[stage, inside] = lax.select(
                    chosen, arrived_ref[stage - 1, plain], carried_ref[stage - 1, inside]
                )
            if stage < hops:
                hop_copy(stage, chunk).start()
            if stage == 0 and chunk + 2 < CHUNKS:
                far_copy(chunk + 2).start()
        if step < CHUNKS:
            multiply(0, lambda index: far_ref[index], step)
            if step == CHUNKS - 1:
                sum_copy(0).start()
        if step >= SLACK * hops:
            multiply(1, lambda index: carried_ref[hops, index], step - SLACK * hops)
    sum_copy(1).start()

    def gathered(which):
        total = products_ref[which, seg] + sums_ref[which]
        return jnp.concatenate(
            [total[coarse * channels : (coarse + 1) * channels] for coarse in range(COARSE)], axis=1
        )

    table = table_ref.reshape(COARSE * width, half * LAGS)
    sum_copy(0).wait_recv()
    from_far = arrange(table, [gathered(0)], factor)
    sum_copy(1).wait_recv()
    from_carried = arrange(table, [gathered(1)], factor)
    out_ref[0] = lax.select(first_far, from_far, from_carried)
    out_ref[1] = lax.select(first_far, from_carried, from_far)
    for chunk in range(CHUNKS):
        far_copy(chunk).wait_send()
        for bit in range(hops):
            hop_copy(bit, chunk).wait_send()
    for which in range(2):
        sum_copy(which).wait_send()


def shards(traces, fir_taps, slot_channel, segment_valid, distances):
    _, channels, samples = traces.shape
    pieces = samples // LANES
    half = channels // 2
    width = FINE * half
    vmem = pl.BlockSpec(memory_space=pltpu.VMEM)
    smem = pl.BlockSpec(memory_space=pltpu.SMEM)
    hbm = pl.BlockSpec(memory_space=pltpu.HBM)
    params = pltpu.CompilerParams(vmem_limit_bytes=64 * 2**20 - 2**17)
    whitened = pl.pallas_call(
        whiten_kernel,
        out_shape=jax.ShapeDtypeStruct((pieces, channels, LANES), jnp.bfloat16),
        in_specs=[hbm] * 4,
        out_specs=vmem,
        scratch_shapes=[
            pltpu.SMEM(slot_channel.shape, jnp.int32),
            pltpu.SMEM(segment_valid.shape, jnp.int32),
            pltpu.VMEM(traces.shape, jnp.bfloat16),
            pltpu.VMEM(fir_taps.shape, jnp.bfloat16),
            pltpu.VMEM(((pieces + 2) * channels, LANES), jnp.float32),
            pltpu.VMEM((channels, 3 * LANES), jnp.float32),
            pltpu.VMEM((pieces * channels, LANES), jnp.float32),
            pltpu.SemaphoreType.DMA((4,)),
        ],
        compiler_params=params,
    )(slot_channel, segment_valid, traces, fir_taps)

    blocks = lax.axis_size("sensor")
    hops = (blocks - 1).bit_length() - 1
    factor = 1.0 / math.sqrt(samples * traces.shape[0] * lax.axis_size("seg"))
    depth = (pieces + 1) * LANES
    return pl.pallas_call(
        functools.partial(exchange_kernel, blocks, factor),
        out_shape=jax.ShapeDtypeStruct((2, channels, half * LAGS), jnp.float32),
        in_specs=[smem, vmem],
        out_specs=vmem,
        scratch_shapes=[
            pltpu.VMEM((pieces + 3, channels, LANES), jnp.bfloat16),
            pltpu.VMEM((pieces + 2, channels, LANES), jnp.bfloat16),
            pltpu.VMEM((hops + 1, pieces + 2, channels, LANES), jnp.bfloat16),
            pltpu.VMEM((hops, pieces, channels, LANES), jnp.bfloat16),
            pltpu.VMEM((COARSE * channels, depth), jnp.bfloat16),
            pltpu.VMEM((2 * width, (pieces // CHUNKS + 1) * LANES), jnp.bfloat16),
            pltpu.VMEM((2, 2, COARSE * channels, width), jnp.float32),
            pltpu.VMEM((2, COARSE * channels, width), jnp.float32),
            pltpu.VMEM((COARSE, width, half * LAGS), jnp.bfloat16),
            pltpu.SemaphoreType.DMA((2, CHUNKS)),
            pltpu.SemaphoreType.DMA((2, hops, CHUNKS)),
            pltpu.SemaphoreType.DMA((2, 2)),
        ],
        compiler_params=pltpu.CompilerParams(
            collective_id=0, has_side_effects=True, vmem_limit_bytes=48 * 2**20
        ),
    )(distances, whitened)


def solution(mesh):
    placed = (
        P("seg", ("groups", "sensor"), None),
        P(("groups", "sensor"), None),
        P(("groups", "sensor"), None),
        P("seg", ("groups", "sensor")),
        P(),
    )
    return jax.shard_map(
        shards,
        mesh=mesh,
        in_specs=placed,
        out_specs=P(None, ("groups", "sensor"), "seg"),
        check_vma=False,
    )
```

```python
import functools
import math

import jax
import jax.numpy as jnp
from jax import lax
from jax.experimental import pallas as pl
from jax.experimental.pallas import tpu as pltpu
from jax.sharding import PartitionSpec as P

LAGS = 48
FINE = 8
COARSE = LAGS // FINE
LANES = 128
CHUNKS = 4
SLACK = 3
EPSILON = 1e-06
NT = (((1,), (1,)), ((), ()))


def whiten_kernel(
    slot_hbm, valid_hbm, traces_hbm, taps_hbm, out_ref, slot_ref, valid_ref, traces_ref, taps_ref,
    rows_ref, taps_f32, scaled_ref, sems,
):
    copies = [
        pltpu.make_async_copy(source, target, sems.at[index])
        for index, (source, target) in enumerate(
            [(traces_hbm, traces_ref), (taps_hbm, taps_ref), (slot_hbm, slot_ref), (valid_hbm, valid_ref)]
        )
    ]
    for copy in copies:
        copy.start()
    for copy in copies:
        copy.wait()
    channels, samples = traces_ref.shape[1:]
    tap_count = taps_ref.shape[1]
    pieces = samples // LANES
    margin = (tap_count - 1) // 2
    width = 3 * LANES
    rows_ref[0:channels] = jnp.zeros((channels, LANES), jnp.float32)
    rows_ref[(pieces + 1) * channels :] = jnp.zeros((channels, LANES), jnp.float32)
    for piece in range(pieces):
        rows_ref[(piece + 1) * channels : (piece + 2) * channels] = traces_ref[
            0, :, piece * LANES : (piece + 1) * LANES
        ].astype(jnp.float32)
    taps_f32[...] = jnp.zeros_like(taps_f32)
    taps_f32[:, 0:tap_count] = taps_ref[...].astype(jnp.float32)

    @pl.loop(0, channels, unroll=8)
    def _(slot):
        channel = slot_ref[0, slot]
        usable = valid_ref[0, channel].astype(jnp.float32)
        windows = jnp.concatenate(
            [
                rows_ref[pl.ds(piece * channels + channel, pieces, stride=channels)].astype(jnp.bfloat16)
                for piece in range(3)
            ],
            axis=1,
        )
        filter_row = jnp.broadcast_to(taps_f32[pl.ds(channel, 1)], (LANES, width))
        banded = pltpu.roll(filter_row, LANES - margin, 1, stride=1, stride_axis=0)
        filtered = lax.dot_general(
            windows, banded.astype(jnp.bfloat16), NT, preferred_element_type=jnp.float32
        )
        energy = jnp.sum(filtered * filtered, keepdims=True) * (1.0 / samples)
        scaled = filtered * (lax.rsqrt(energy + EPSILON) * usable)
        scaled_ref[pl.ds(slot, pieces, stride=channels)] = scaled

    for piece in range(pieces):
        out_ref[piece] = scaled_ref[piece * channels : (piece + 1) * channels].astype(jnp.bfloat16)


def shifted(now, following, amount):
    if amount == 0:
        return now
    lane = lax.broadcasted_iota(jnp.int32, now.shape, 1)
    rolled = [pltpu.roll(x, LANES - amount, 1) for x in (now, following)]
    return jnp.where(lane < LANES - amount, rolled[0], rolled[1])


def arrange(table_ref, parts, factor):
    rows = jnp.concatenate(parts, axis=0) * factor
    top = rows.astype(jnp.bfloat16)
    rest = rows - top.astype(jnp.float32)
    middle = rest.astype(jnp.bfloat16)
    low = (rest - middle.astype(jnp.float32)).astype(jnp.bfloat16)
    stacked = jnp.concatenate([top, middle, low], axis=0)
    moved = jnp.dot(stacked, table_ref[...], preferred_element_type=jnp.float32)
    count = rows.shape[0]
    return moved[:count] + (moved[count : 2 * count] + moved[2 * count :])


def exchange_kernel(
    blocks, factor, distances_ref, own_ref, out_ref, padded_ref, far_ref, carried_ref, arrived_ref,
    left_ref, right_ref, products_ref, sums_ref, table_ref, far_sems, hop_sems, sum_sems,
):
    pieces, channels, _ = own_ref.shape
    half = channels // 2
    before = LAGS // 2
    width = FINE * half
    farthest = blocks - 1
    hops = farthest.bit_length() - 1
    per_chunk = pieces // CHUNKS
    me = lax.axis_index("sensor")
    seg = lax.axis_index("seg")

    def partner(mask):
        result = 0
        for bit in range(farthest.bit_length()):
            value = lax.rem(lax.div(me, 1 << bit), 2)
            result = result + ((1 - value) if (mask >> bit) & 1 else value) * (1 << bit)
        return {"sensor": result}

    barrier = pltpu.get_barrier_semaphore()
    others = [partner(farthest)] + [partner(1 << bit) for bit in range(hops)] + [{"seg": 1 - seg}]
    for other in others:
        pl.semaphore_signal(barrier, inc=1, device_id=other, device_id_type=pl.DeviceIdType.MESH)
    pl.semaphore_wait(barrier, len(others))

    def far_copy(chunk):
        return pltpu.make_async_remote_copy(
            src_ref=own_ref.at[pl.ds(chunk * per_chunk, per_chunk)],
            dst_ref=far_ref.at[pl.ds(1 + chunk * per_chunk, per_chunk)],
            send_sem=far_sems.at[0, chunk],
            recv_sem=far_sems.at[1, chunk],
            device_id=others[0],
            device_id_type=pl.DeviceIdType.MESH,
        )

    def hop_partner(bit):
        up, down = others[1 + bit]["sensor"], others[hops - bit]["sensor"]
        return {"sensor": up + seg * (down - up)}

    def hop_copy(bit, chunk):
        return pltpu.make_async_remote_copy(
            src_ref=carried_ref.at[bit, pl.ds(1 + chunk * per_chunk, per_chunk)],
            dst_ref=arrived_ref.at[bit, pl.ds(chunk * per_chunk, per_chunk)],
            send_sem=hop_sems.at[0, bit, chunk],
            recv_sem=hop_sems.at[1, bit, chunk],
            device_id=hop_partner(bit),
            device_id_type=pl.DeviceIdType.MESH,
        )

    def sum_copy(which):
        return pltpu.make_async_remote_copy(
            src_ref=products_ref.at[which, 1 - seg],
            dst_ref=sums_ref.at[which],
            send_sem=sum_sems.at[0, which],
            recv_sem=sum_sems.at[1, which],
            device_id=others[-1],
            device_id_type=pl.DeviceIdType.MESH,
        )

    for chunk in range(min(2, CHUNKS)):
        far_copy(chunk).start()

    first_far = distances_ref[0] == farthest
    distance = jnp.where(first_far, distances_ref[1], distances_ref[0])
    crosses = distance >= blocks // 2
    remaining = jnp.where(crosses, farthest - distance, distance)

    edge = jnp.zeros((channels, LANES), jnp.bfloat16)
    padded_ref[0] = edge
    padded_ref[1] = edge
    padded_ref[pieces + 2] = edge
    far_ref[0] = edge
    far_ref[pieces + 1] = edge
    carried_ref[hops, 0] = edge
    carried_ref[hops, pieces + 1] = edge

    @pl.loop(0, pieces)
    def _(piece):
        padded_ref[piece + 2] = own_ref[piece]

    @pl.loop(0, pieces + 1, unroll=3)
    def _(piece):
        lanes = pl.ds(pl.multiple_of(piece * LANES, LANES), LANES)
        last, now, later = (padded_ref[piece + step].astype(jnp.float32) for step in range(3))
        for coarse in range(COARSE):
            amount = before - FINE * coarse
            if amount >= 0:
                value = shifted(now, later, amount)
            else:
                value = shifted(last, now, LANES + amount)
            left_ref[coarse * channels : (coarse + 1) * channels, lanes] = value.astype(jnp.bfloat16)

    for coarse in range(COARSE):
        row = lax.broadcasted_iota(jnp.int32, table_ref.shape[1:], 0)
        column = lax.broadcasted_iota(jnp.int32, table_ref.shape[1:], 1)
        target = (row & (half - 1)) * LAGS + (row >> (half.bit_length() - 1)) + coarse * FINE
        table_ref[coarse] = jnp.where(column == target, 1.0, 0.0).astype(jnp.bfloat16)

    def multiply(which, load, chunk):
        start = chunk * per_chunk
        count = per_chunk + (1 if chunk == CHUNKS - 1 else 0)

        @pl.loop(0, count, unroll=count)
        def _(step):
            lanes = pl.ds(pl.multiple_of(step * LANES, LANES), LANES)
            now, later = (load(start + step + ahead).astype(jnp.float32) for ahead in range(2))
            for fine in range(FINE):
                value = shifted(now, later, fine).astype(jnp.bfloat16)
                for part in range(2):
                    row = part * width + fine * half
                    right_ref[row : row + half, lanes] = value[part * half : (part + 1) * half]

        product = lax.dot_general(
            left_ref[:, start * LANES : (start + count) * LANES],
            right_ref[:, : count * LANES],
            NT,
            preferred_element_type=jnp.float32,
        )
        for part in range(2):
            addend = product[:, part * width : (part + 1) * width]
            if chunk == 0:
                products_ref[which, part] = addend
            else:
                products_ref[which, part] += addend

    for step in range(CHUNKS + SLACK * hops):
        for stage in range(hops, -1, -1):
            chunk = step - SLACK * stage
            if chunk < 0 or chunk >= CHUNKS:
                continue
            inside = pl.ds(1 + chunk * per_chunk, per_chunk)
            plain = pl.ds(chunk * per_chunk, per_chunk)
            if stage == 0:
                far_copy(chunk).wait_recv()
                carried_ref[0, inside] = lax.select(crosses, far_ref[inside], own_ref[plain])
            else:
                hop_copy(stage - 1, chunk).wait_recv()
                chosen = jnp.bitwise_and(jnp.right_shift(remaining, stage - 1 + seg * (hops + 1 - 2 * stage)), 1) == 1
                carried_ref[stage, inside] = lax.select(
                    chosen, arrived_ref[stage - 1, plain], carried_ref[stage - 1, inside]
                )
            if stage < hops:
                hop_copy(stage, chunk).start()
            if stage == 0 and chunk + 2 < CHUNKS:
                far_copy(chunk + 2).start()
        if step < CHUNKS:
            multiply(0, lambda index: far_ref[index], step)
            if step == CHUNKS - 1:
                sum_copy(0).start()
        if step >= SLACK * hops:
            multiply(1, lambda index: carried_ref[hops, index], step - SLACK * hops)
    sum_copy(1).start()

    def gathered(which):
        total = products_ref[which, seg] + sums_ref[which]
        return jnp.concatenate(
            [total[coarse * channels : (coarse + 1) * channels] for coarse in range(COARSE)], axis=1
        )

    table = table_ref.reshape(COARSE * width, half * LAGS)
    sum_copy(0).wait_recv()
    from_far = arrange(table, [gathered(0)], factor)
    sum_copy(1).wait_recv()
    from_carried = arrange(table, [gathered(1)], factor)
    out_ref[0] = lax.select(first_far, from_far, from_carried)
    out_ref[1] = lax.select(first_far, from_carried, from_far)
    for chunk in range(CHUNKS):
        far_copy(chunk).wait_send()
        for bit in range(hops):
            hop_copy(bit, chunk).wait_send()
    for which in range(2):
        sum_copy(which).wait_send()


def shards(traces, fir_taps, slot_channel, segment_valid, distances):
    _, channels, samples = traces.shape
    pieces = samples // LANES
    half = channels // 2
    width = FINE * half
    vmem = pl.BlockSpec(memory_space=pltpu.VMEM)
    smem = pl.BlockSpec(memory_space=pltpu.SMEM)
    hbm = pl.BlockSpec(memory_space=pltpu.HBM)
    params = pltpu.CompilerParams(vmem_limit_bytes=64 * 2**20 - 2**17)
    whitened = pl.pallas_call(
        whiten_kernel,
        out_shape=jax.ShapeDtypeStruct((pieces, channels, LANES), jnp.bfloat16),
        in_specs=[hbm] * 4,
        out_specs=vmem,
        scratch_shapes=[
            pltpu.SMEM(slot_channel.shape, jnp.int32),
            pltpu.SMEM(segment_valid.shape, jnp.int32),
            pltpu.VMEM(traces.shape, jnp.bfloat16),
            pltpu.VMEM(fir_taps.shape, jnp.bfloat16),
            pltpu.VMEM(((pieces + 2) * channels, LANES), jnp.float32),
            pltpu.VMEM((channels, 3 * LANES), jnp.float32),
            pltpu.VMEM((pieces * channels, LANES), jnp.float32),
            pltpu.SemaphoreType.DMA((4,)),
        ],
        compiler_params=params,
    )(slot_channel, segment_valid, traces, fir_taps)

    blocks = lax.axis_size("sensor")
    hops = (blocks - 1).bit_length() - 1
    factor = 1.0 / math.sqrt(samples * traces.shape[0] * lax.axis_size("seg"))
    depth = (pieces + 1) * LANES
    return pl.pallas_call(
        functools.partial(exchange_kernel, blocks, factor),
        out_shape=jax.ShapeDtypeStruct((2, channels, half * LAGS), jnp.float32),
        in_specs=[smem, vmem],
        out_specs=vmem,
        scratch_shapes=[
            pltpu.VMEM((pieces + 3, channels, LANES), jnp.bfloat16),
            pltpu.VMEM((pieces + 2, channels, LANES), jnp.bfloat16),
            pltpu.VMEM((hops + 1, pieces + 2, channels, LANES), jnp.bfloat16),
            pltpu.VMEM((hops, pieces, channels, LANES), jnp.bfloat16),
            pltpu.VMEM((COARSE * channels, depth), jnp.bfloat16),
            pltpu.VMEM((2 * width, (pieces // CHUNKS + 1) * LANES), jnp.bfloat16),
            pltpu.VMEM((2, 2, COARSE * channels, width), jnp.float32),
            pltpu.VMEM((2, COARSE * channels, width), jnp.float32),
            pltpu.VMEM((COARSE, width, half * LAGS), jnp.bfloat16),
            pltpu.SemaphoreType.DMA((2, CHUNKS)),
            pltpu.SemaphoreType.DMA((2, hops, CHUNKS)),
            pltpu.SemaphoreType.DMA((2, 2)),
        ],
        compiler_params=pltpu.CompilerParams(
            collective_id=0, has_side_effects=True, vmem_limit_bytes=48 * 2**20
        ),
    )(distances, whitened)


def solution(mesh):
    placed = (
        P("seg", ("groups", "sensor"), None),
        P(("groups", "sensor"), None),
        P(("groups", "sensor"), None),
        P("seg", ("groups", "sensor")),
        P(),
    )
    return jax.shard_map(
        shards,
        mesh=mesh,
        in_specs=placed,
        out_specs=P(None, ("groups", "sensor"), "seg"),
        check_vma=False,
    )
```
